32 devices in a mesh: groups: 2 (over y), blocks: 4 (over z), pairs: 2 (over x), sub: 2 (over core).
Axes of the slice: x: 2, y: 2, z: 4, core: 2. Of those that a mesh axis runs over, the one named last changes fastest.
Arguments:
- coords: float32 [3, 131072], P(None, ('groups', 'blocks')), parts along dimension 1, may hold values from 0 to 132, as said below
- probes: float32 [8, 131072], P(None, ('groups', 'blocks')), parts along dimension 1, may hold values from -6 to 6
- noise: float32 [131072], P(('groups', 'blocks')), parts along dimension 0, may hold values from 0.2 to 1
- pair_list: int32 [2, 6144], P(None, ('groups', 'blocks', 'pairs', 'sub')), parts along dimension 1, may hold values from 0 to 255, as said below
- pair_count: int32 [32], P(('groups', 'blocks', 'pairs', 'sub')), parts along dimension 0, may hold values from 1 to 192
- coeffs: float32 [10], P('groups'), parts along dimension 0, may hold values from 0.5 to 1.5
Outputs:
- poly_probes: float32 [8, 131072], P(None, ('groups', 'blocks')), parts along dimension 1
The draws below stay inside these ranges and needn't reach their ends.
There are 2 independent parts, one for each index of `groups`. The reference program is written for one: setup_inputs(seed, part) draws one part's arguments, and reference() takes and returns one part's arrays. A program takes and returns all parts, laid end to end along the dimension named above; each array names one. Nothing has to cross between parts.
Inputs may be any that keep to these rules, and one draw needn't show every extreme that they name: `pair_list`: the list of slot s belongs to index b = s // 768 of blocks; its first block i lies in b * 64 to (b + 1) * 64 - 1, and i <= j < i + 8. Slots past the count hold pairs too, which are not used. A pair may be listed more than once; each live listing counts. `coords`: rows x, y, z. The points of block k lie within x from k / 2 to k / 2 + 3.5, and y, z from 0 to 3.
All inputs are finite; a program needn't handle non-finite values.
Results may differ from the reference program's by a relative error of at most 0.00019.
Values sent between devices are 32-bit elements; how exact they have to be, the bound alone decides.
A program may use at most 192 MiB of HBM per device.

```python
import math
import jax
import jax.numpy as jnp
from jax import lax

PTS_BLK = 256
PROBES = 8
BLK_DEV = 64
REACH = 8
DEG = 4
NBLK = 256
NPTS = 65536
LISTS_GRP = 4
LISTS = 16
PAIR_CAP = 192
SLOTS = 3072


def draw_coords(key, part):
    key = jax.random.fold_in(key, 11)
    spread = jax.random.uniform(key, (3, NPTS), jnp.float32)
    block_ids = (jnp.arange(NPTS, dtype=jnp.int32) // PTS_BLK).astype(jnp.float32)
    xcoord = block_ids * 0.5 + 3.5 * spread[0]
    ycoord = 3.0 * spread[1]
    zcoord = 3.0 * spread[2]
    return jnp.stack([xcoord, ycoord, zcoord]).astype(jnp.float32)


def draw_pair_list(key, part):
    key = jax.random.fold_in(key, 23)
    first_key, second_key = jax.random.split(key)
    slot_ids = jnp.arange(SLOTS, dtype=jnp.int32)
    owner = slot_ids // (PAIR_CAP * LISTS_GRP)
    first = owner * BLK_DEV + jax.random.randint(first_key, (SLOTS,), 0, BLK_DEV, jnp.int32)
    offset = jax.random.randint(second_key, (SLOTS,), 0, REACH, jnp.int32)
    second = jnp.minimum(first + offset, NBLK - 1)
    return jnp.stack([first, second]).astype(jnp.int32)


def draw_pair_count(key, part):
    key = jax.random.fold_in(key, 37)
    count_key, chosen_key = jax.random.split(key)
    counts = jax.random.randint(count_key, (LISTS,), PAIR_CAP // 2, PAIR_CAP + 1, jnp.int32)
    owners = LISTS // LISTS_GRP
    chosen = jax.random.randint(chosen_key, (owners,), 0, LISTS_GRP, jnp.int32)
    list_ids = jnp.arange(LISTS, dtype=jnp.int32)
    full = list_ids % LISTS_GRP == chosen[list_ids // LISTS_GRP]
    return jnp.where(full, PAIR_CAP, counts).astype(jnp.int32)


def shard_levels(key, shape, cuts, smallest, top_value):
    factor_of, own = 1.0, jax.random.fold_in(key, 6)
    for position, blocks in cuts:
        draws = jnp.exp(jax.random.uniform(jax.random.fold_in(own, position), (blocks,), jnp.float32, smallest / len(cuts), top_value / len(cuts)))
        factor_of = factor_of * jnp.repeat(draws, shape[position] // blocks).reshape([-1 if axis == position else 1 for axis in range(len(shape))])
    return factor_of


def bell_draw(own_key, dims, deviation, reach, cuts=(), kind=jnp.bfloat16):
    entries = jax.random.normal(own_key, dims, jnp.float32) * deviation
    if len(cuts) > 0:
        entries = shard_levels(own_key, dims, cuts, -0.22, 0.18) * entries
    return jnp.clip(entries, min=-reach, max=reach).astype(kind)


def setup_inputs(seed: int = 0, part: int = 0) -> dict:
    arg_keys = jax.random.split(jax.random.key(seed), 7)
    part_keys = jax.random.split(jax.random.fold_in(arg_keys[6], part), 7)
    return {
        "coords": draw_coords(jax.random.fold_in(jax.random.fold_in(arg_keys[6], part), 71), part),
        "probes": bell_draw(part_keys[1], (PROBES, NPTS), 1.0, 6.0, ((1, 4),), jnp.float32),
        "noise": jnp.clip(jnp.exp(math.log(1.0) - 1.609438 * jax.random.uniform(part_keys[2], (NPTS,), jnp.float32) ** shard_levels(part_keys[2], (NPTS,), ((0, 4),), -0.2, 0.2)), 0.2, 1.0),
        "pair_list": draw_pair_list(jax.random.fold_in(jax.random.fold_in(arg_keys[6], part), 71), part),
        "pair_count": draw_pair_count(jax.random.fold_in(jax.random.fold_in(arg_keys[6], part), 71), part),
        "coeffs": jnp.clip(jax.random.uniform(part_keys[5], (DEG + 1,), jnp.float32, 0.5, 1.5), 0.5, 1.5),
    }


kernel_scale = 0.1
spectrum_center = 1.0
spectrum_half = 2.0

def wendland(first, second):
    diff = first[:, :, :, None] - second[:, :, None, :]
    dist = jnp.sqrt(lax.optimization_barrier(jnp.sum(diff * diff, axis=0)))
    inside = jnp.maximum(1.0 - dist, 0.0)
    return kernel_scale * inside ** 4 * (4.0 * dist + 1.0)

def reference(coords, probes, noise, pair_list, pair_count, coeffs):
    points = coords.reshape(3, NBLK, PTS_BLK)
    slot_ids = jnp.arange(SLOTS, dtype=jnp.int32)
    live = slot_ids % PAIR_CAP < pair_count[slot_ids // PAIR_CAP]
    rows = pair_list[0]
    cols = pair_list[1]
    weight_fwd = live.astype(jnp.float32)
    weight_back = (live & (rows != cols)).astype(jnp.float32)
    group = math.gcd(SLOTS, 64)
    turns = SLOTS // group
    items = (rows.reshape(turns, group), cols.reshape(turns, group), weight_fwd.reshape(turns, group), weight_back.reshape(turns, group))

    def apply_kernel(vec):
        blocked = vec.reshape(PROBES, NBLK, PTS_BLK)

        def step(acc, item):
            row_ids, col_ids, wf, wb = item
            tile = wendland(points[:, row_ids], points[:, col_ids])
            fwd = jnp.einsum('gab,qgb->gqa', tile, blocked[:, col_ids], precision=lax.Precision.HIGHEST)
            bwd = jnp.einsum('gab,qga->gqb', tile, blocked[:, row_ids], precision=lax.Precision.HIGHEST)
            fwd = fwd * wf[:, None, None]
            bwd = bwd * wb[:, None, None]
            acc = acc.at[:, row_ids].add(jnp.transpose(fwd, (1, 0, 2)))
            acc = acc.at[:, col_ids].add(jnp.transpose(bwd, (1, 0, 2)))
            return (acc, None)
        acc, _ = lax.scan(step, jnp.zeros((PROBES, NBLK, PTS_BLK), jnp.float32), items)
        return noise[None, :] * vec + acc.reshape(PROBES, NPTS)

    def scaled(vec):
        return (apply_kernel(vec) - spectrum_center * vec) / spectrum_half
    previous = probes
    current = scaled(probes)
    total = coeffs[0] * previous + coeffs[1] * current
    for order in range(2, DEG + 1):
        following = 2.0 * scaled(current) - previous
        total = total + coeffs[order] * following
        previous = current
        current = following
    return total
```

```python
import functools

import jax
import jax.numpy as jnp
from jax import lax
from jax.experimental import pallas as pl
from jax.experimental.pallas import tpu as pltpu
from jax.sharding import PartitionSpec as P

PTS_BLK = 256
REACH = 8
DEG = 4
HALO = REACH - 1
PROBES = 8

kernel_scale = 0.1
spectrum_center = 1.0
spectrum_half = 2.0

MESH = pl.DeviceIdType.MESH


def rounded(value):
    return value.astype(jnp.bfloat16).astype(jnp.float32)


def pieces(value):
    first = rounded(value)
    second = rounded(value - first)
    return first, second, rounded(value - first - second)


def stacked(value):
    high = rounded(value)
    return jnp.concatenate([high, value - high], 0).astype(jnp.bfloat16)


def kernel(
    layout,
    coords_ref,
    probes_ref,
    noise_ref,
    list_ref,
    count_ref,
    coeffs_ref,
    out_ref,
    pts,
    vec_a,
    vec_b,
    acc,
    arrived,
    keys,
    weights,
    tile_hi,
    tile_lo,
    pts_send,
    pts_recv,
    halo_send,
    halo_recv,
    term_send,
    term_recv,
    key_send,
    key_recv,
    out_send,
    out_recv,
):
    blocks, pairs, sub, split_sub, blocks_here = layout
    width = sub if split_sub else 1
    chain = pairs * width
    own = blocks_here // chain
    own_pts = own * PTS_BLK
    rim_pts = HALO * PTS_BLK
    window = REACH * PTS_BLK
    g = lax.axis_index("groups")
    b = lax.axis_index("blocks")
    p = lax.axis_index("pairs")
    s = lax.axis_index("sub")

    def position(b, p, s):
        lane = s + lax.rem(p, 2) * (sub - 1 - 2 * s) if split_sub else 0
        along = p * width + lane
        return along + lax.rem(b, 2) * (chain - 1 - 2 * along)

    def device(rank):
        at_b = lax.div(rank, chain)
        q = lax.rem(rank, chain)
        along = q + lax.rem(at_b, 2) * (chain - 1 - 2 * q)
        at_p = lax.div(along, width)
        lane = lax.rem(along, width)
        at_s = lane + lax.rem(at_p, 2) * (sub - 1 - 2 * lane) if split_sub else s
        return (g, at_b, at_p, at_s)

    q = position(b, p, s)
    rank = b * chain + q
    has_next = rank < blocks * chain - 1
    has_prev = rank > 0
    following = device(jnp.minimum(rank + 1, blocks * chain - 1))
    preceding = device(jnp.maximum(rank - 1, 0))
    member = p * sub + s
    members = pairs * sub

    def other(step):
        there = lax.rem(member + step, members)
        return (g, b, lax.div(there, sub), lax.rem(there, sub))

    here = pl.ds(pl.multiple_of(q * own_pts, PTS_BLK), own_pts)
    pts[...] = jnp.zeros_like(pts)
    pts[0:3, 0:own_pts] = coords_ref[:, here]
    vec_a[:, 0:own_pts] = probes_ref[:, here]
    vec_a[:, own_pts:] = jnp.zeros((PROBES, rim_pts), jnp.float32)
    vec_b[:, own_pts:] = jnp.zeros((PROBES, rim_pts), jnp.float32)
    cap = list_ref.shape[1]
    slot_ids = lax.broadcasted_iota(jnp.int32, (1, cap), 1)
    first_of = list_ref[0:1, :]
    key = (first_of - b * blocks_here) * REACH + list_ref[1:2, :] - first_of
    my_keys = keys.at[member]
    my_keys[...] = jnp.full(my_keys.shape, -1, jnp.int32)
    my_keys[0:1, 0:cap] = jnp.where(slot_ids < count_ref[0], key, -1)

    barrier = pltpu.get_barrier_semaphore()
    cross_next = (q == chain - 1) & has_next
    cross_prev = (q == 0) & has_prev
    for step in range(1, members):
        pl.semaphore_signal(barrier, inc=1, device_id=other(step), device_id_type=MESH)

    @pl.when(cross_next)
    def _():
        pl.semaphore_signal(barrier, inc=1, device_id=following, device_id_type=MESH)

    @pl.when(cross_prev)
    def _():
        pl.semaphore_signal(barrier, inc=1, device_id=preceding, device_id_type=MESH)

    greeted = members - 1 + cross_next.astype(jnp.int32) + cross_prev.astype(jnp.int32)
    pl.semaphore_wait(barrier, greeted)

    def rim_copy(buffer, send, recv):
        return pltpu.make_async_remote_copy(
            src_ref=buffer.at[:, pl.ds(0, rim_pts)],
            dst_ref=buffer.at[:, pl.ds(own_pts, rim_pts)],
            send_sem=send,
            recv_sem=recv,
            device_id=preceding,
            device_id_type=MESH,
        )

    def term_copy(order):
        return pltpu.make_async_remote_copy(
            src_ref=acc.at[:, pl.ds(own_pts, rim_pts)],
            dst_ref=arrived,
            send_sem=term_send.at[order],
            recv_sem=term_recv.at[order],
            device_id=following,
            device_id_type=MESH,
        )

    pts_copy = rim_copy(pts, pts_send, pts_recv)
    halo_copies = [
        rim_copy((vec_a, vec_b)[k % 2], halo_send.at[k], halo_recv.at[k]) for k in range(DEG)
    ]
    term_copies = [term_copy(k) for k in range(DEG)]
    key_copies = [
        pltpu.make_async_remote_copy(
            src_ref=my_keys,
            dst_ref=my_keys,
            send_sem=key_send.at[step],
            recv_sem=key_recv.at[step],
            device_id=other(step),
            device_id_type=MESH,
        )
        for step in range(1, members)
    ]

    @pl.when(has_prev)
    def _():
        pts_copy.start()
        halo_copies[0].start()

    for copy in key_copies:
        copy.start()

    row8 = lax.broadcasted_iota(jnp.int32, (8, 1), 0)

    def build_row(i, carry):
        start = pl.multiple_of(i * PTS_BLK, PTS_BLK)
        block_id = b * blocks_here + q * own + i
        middle = block_id.astype(jnp.float32) * 0.5 + 2.0
        centre = jnp.where(row8 == 0, middle, jnp.where(row8 < 3, 1.5, 0.0))
        local = pts[:, pl.ds(start, window)] - centre
        norm = jnp.sum(local * local, axis=0, keepdims=True)
        b0, b1, b2 = pieces(jnp.where(row8 == 4, norm, local))
        right = jnp.concatenate(
            [
                jnp.where(row8 == 3, 1.0, b0),
                jnp.where(row8 == 3, 1.0, b1),
                jnp.where(row8 < 3, b0, jnp.where(row8 == 3, 1.0, b2)),
                b1,
                b2,
                b0,
            ],
            0,
        ).astype(jnp.bfloat16)
        a0, a1, a2 = pieces(
            jnp.where(row8 == 3, norm[:, :PTS_BLK], -2.0 * local[:, :PTS_BLK])
        )
        left = jnp.concatenate(
            [
                jnp.where(row8 == 4, 1.0, a0),
                jnp.where(row8 < 3, a0, jnp.where(row8 == 4, 1.0, a1)),
                jnp.where(row8 < 3, a1, jnp.where(row8 == 4, 1.0, a2)),
                jnp.where(row8 < 3, a1, 0.0),
                jnp.where(row8 < 3, a0, 0.0),
                jnp.where(row8 < 3, a2, 0.0),
            ],
            0,
        )
        left = left.T.astype(jnp.bfloat16)
        for d in range(REACH):
            columns = slice(d * PTS_BLK, (d + 1) * PTS_BLK)
            square = jnp.dot(left, right[:, columns], preferred_element_type=jnp.float32)
            square = jnp.maximum(square, 1e-12)
            inside = jnp.maximum(1.0 - square * lax.rsqrt(square), 0.0)
            inside2 = inside * inside
            tile = (inside2 * inside2) * (5.0 * kernel_scale - 4.0 * kernel_scale * inside)
            high = tile.astype(jnp.bfloat16)
            tile_hi[i, :, columns] = high
            tile_lo[i, :, columns] = (tile - high.astype(jnp.float32)).astype(jnp.bfloat16)
        return carry

    inner = own - HALO
    lax.fori_loop(0, inner, build_row, 0)

    @pl.when(has_next)
    def _():
        pts_copy.wait_recv()

    lax.fori_loop(inner, own, build_row, 0)

    for copy in key_copies:
        copy.wait_recv()
    own_rows = lax.broadcasted_iota(jnp.int32, (own, 1), 0)
    for d in range(REACH):
        ids = (q * own + own_rows) * REACH + d
        count = jnp.zeros((own, 1), jnp.float32)
        for m in range(members):
            same = jnp.where(keys[m, 0:1, :] == ids, 1.0, 0.0)
            count = count + jnp.sum(same, axis=1, keepdims=True)
        weights[:, d * PTS_BLK : (d + 1) * PTS_BLK] = jnp.broadcast_to(count, (own, PTS_BLK))

    off_diagonal = lax.broadcasted_iota(jnp.int32, (1, window), 1) >= PTS_BLK

    def apply_rows(current):
        def body(i, carry):
            start = pl.multiple_of(i * PTS_BLK, PTS_BLK)
            weight = weights[pl.ds(i, 1), :]
            reach = pl.ds(start, window)
            block = pl.ds(start, PTS_BLK)
            seen = stacked(current[:, reach] * weight)
            mine = stacked(current[:, block])
            by_last = (((1,), (1,)), ((), ()))
            fwd = lax.dot_general(seen, tile_hi[i], by_last, preferred_element_type=jnp.float32)
            fwd += lax.dot_general(seen, tile_lo[i], by_last, preferred_element_type=jnp.float32)
            bwd = jnp.dot(mine, tile_hi[i], preferred_element_type=jnp.float32)
            bwd += jnp.dot(mine, tile_lo[i], preferred_element_type=jnp.float32)
            back = (bwd[:PROBES] + bwd[PROBES:]) * jnp.where(off_diagonal, weight, 0.0)
            acc[:, reach] += back
            acc[:, block] += fwd[:PROBES] + fwd[PROBES:]
            return carry

        return body

    early = (inner + 1) // 2
    for k in range(DEG):
        current = (vec_a, vec_b)[k % 2]
        before = (vec_b, vec_a)[k % 2]
        body = apply_rows(current)
        acc[...] = jnp.zeros_like(acc)
        lax.fori_loop(0, early, body, 0)

        @pl.when(has_next)
        def _():
            halo_copies[k].wait_recv()

        lax.fori_loop(inner, own, body, 0)

        @pl.when(has_next)
        def _():
            term_copies[k].start()

        lax.fori_loop(early, inner, body, 0)

        @pl.when(has_prev)
        def _():
            halo_copies[k].wait_send()
            term_copies[k].wait_recv()
            acc[:, 0:rim_pts] += arrived[...]

        def advance(lo, hi):
            at = pl.ds(pl.multiple_of(q * own_pts + lo, PTS_BLK), hi - lo)
            value = current[:, lo:hi]
            moved = noise_ref[:, at] * value + acc[:, lo:hi] - spectrum_center * value
            if k == 0:
                fresh = moved / spectrum_half
                out_ref[:, at] = coeffs_ref[0] * value + coeffs_ref[1] * fresh
            else:
                fresh = moved * (2.0 / spectrum_half) - before[:, lo:hi]
                out_ref[:, at] = out_ref[:, at] + coeffs_ref[k + 1] * fresh
            if k < DEG - 1:
                before[:, lo:hi] = fresh

        advance(0, rim_pts)
        if k < DEG - 1:

            @pl.when(has_prev)
            def _():
                halo_copies[k + 1].start()

        advance(rim_pts, own_pts)

        @pl.when(has_next)
        def _():
            term_copies[k].wait_send()

    @pl.when(has_prev)
    def _():
        pts_copy.wait_send()

    for copy in key_copies:
        copy.wait_send()

    def out_copy(at_p, sem, device_id):
        at_q = position(b, at_p, s)
        part = out_ref.at[:, pl.ds(pl.multiple_of(at_q * own_pts, PTS_BLK), own_pts)]
        return pltpu.make_async_remote_copy(
            src_ref=part,
            dst_ref=part,
            send_sem=out_send.at[sem],
            recv_sem=out_recv.at[sem],
            device_id=device_id,
            device_id_type=MESH,
        )

    across = [out_copy(p, step, (g, b, lax.rem(p + step, pairs), s)) for step in range(1, pairs)]
    for copy in across:
        copy.start()
    inside = []
    if split_sub:
        for step in range(pairs):
            if step > 0:
                across[step - 1].wait_recv()
            source = lax.rem(p + pairs - step, pairs)
            for turn in range(1, sub):
                sem = pairs + step * sub + turn
                copy = out_copy(source, sem, (g, b, p, lax.rem(s + turn, sub)))
                copy.start()
                inside.append(copy)
    else:
        for copy in across:
            copy.wait_recv()
    for copy in inside:
        copy.wait_recv()
    for copy in across + inside:
        copy.wait_send()


def on_device(layout, coords, probes, noise, pair_list, pair_count, coeffs):
    blocks, pairs, sub, split_sub, blocks_here = layout
    own = blocks_here // (pairs * (sub if split_sub else 1))
    members = pairs * sub
    own_pts = own * PTS_BLK
    ext_pts = own_pts + HALO * PTS_BLK
    window = REACH * PTS_BLK
    key_lanes = -(-pair_list.shape[1] // 128) * 128
    dma = pltpu.SemaphoreType.DMA
    vmem = pl.BlockSpec(memory_space=pltpu.VMEM)
    smem = pl.BlockSpec(memory_space=pltpu.SMEM)
    return pl.pallas_call(
        functools.partial(kernel, layout),
        out_shape=jax.ShapeDtypeStruct(probes.shape, jnp.float32),
        in_specs=[vmem, vmem, vmem, vmem, smem, smem],
        out_specs=vmem,
        scratch_shapes=[
            pltpu.VMEM((8, ext_pts), jnp.float32),
            pltpu.VMEM((PROBES, ext_pts), jnp.float32),
            pltpu.VMEM((PROBES, ext_pts), jnp.float32),
            pltpu.VMEM((PROBES, ext_pts), jnp.float32),
            pltpu.VMEM((PROBES, HALO * PTS_BLK), jnp.float32),
            pltpu.VMEM((members, 8, key_lanes), jnp.int32),
            pltpu.VMEM((own, window), jnp.float32),
            pltpu.VMEM((own, PTS_BLK, window), jnp.bfloat16),
            pltpu.VMEM((own, PTS_BLK, window), jnp.bfloat16),
            dma,
            dma,
            dma((DEG,)),
            dma((DEG,)),
            dma((DEG,)),
            dma((DEG,)),
            dma((members,)),
            dma((members,)),
            dma((pairs + members,)),
            dma((pairs + members,)),
        ],
        compiler_params=pltpu.CompilerParams(
            collective_id=0, has_side_effects=True, vmem_limit_bytes=56 * 1024 * 1024
        ),
    )(coords, probes, noise.reshape(1, -1), pair_list, pair_count, coeffs)


def solution(mesh):
    blocks, pairs, sub = (mesh.shape[axis] for axis in ("blocks", "pairs", "sub"))

    def program(coords, *rest):
        total = coords.shape[1] // PTS_BLK
        blocks_here = total // (mesh.shape["groups"] * blocks)
        split_sub = blocks_here // (pairs * sub) >= REACH
        layout = (blocks, pairs, sub, split_sub, blocks_here)
        return jax.shard_map(
            functools.partial(on_device, layout),
            mesh=mesh,
            in_specs=(
                P(None, ("groups", "blocks")),
                P(None, ("groups", "blocks")),
                P(("groups", "blocks")),
                P(None, ("groups", "blocks", "pairs", "sub")),
                P(("groups", "blocks", "pairs", "sub")),
                P("groups"),
            ),
            out_specs=P(None, ("groups", "blocks")),
            check_vma=False,
        )(coords, *rest)

    return program
```

```python
import functools

import jax
import jax.numpy as jnp
from jax import lax
from jax.experimental import pallas as pl
from jax.experimental.pallas import tpu as pltpu
from jax.sharding import PartitionSpec as P

PTS_BLK = 256
REACH = 8
DEG = 4
HALO = REACH - 1
PROBES = 8

kernel_scale = 0.1
spectrum_center = 1.0
spectrum_half = 2.0

MESH = pl.DeviceIdType.MESH

TILE_UNIT = 2.0**20
STRETCH = (4.0 * kernel_scale * TILE_UNIT) ** 0.2
TOP = 240.0


def rounded(value):
    return value.astype(jnp.bfloat16).astype(jnp.float32)


def pieces(value):
    first = rounded(value)
    second = rounded(value - first)
    return first, second, rounded(value - first - second)


def stacked(value):
    high = rounded(value)
    return jnp.concatenate([high, value - high], 0).astype(jnp.bfloat16)


def kernel(
    layout,
    coords_ref,
    probes_ref,
    noise_ref,
    list_ref,
    count_ref,
    coeffs_ref,
    out_ref,
    pts,
    vec_a,
    vec_b,
    acc,
    arrived,
    keys,
    weights,
    tile_hi,
    tile_lo,
    pts_send,
    pts_recv,
    halo_send,
    halo_recv,
    term_send,
    term_recv,
    key_send,
    key_recv,
    out_send,
    out_recv,
):
    blocks, pairs, sub, split_sub, blocks_here = layout
    width = sub if split_sub else 1
    chain = pairs * width
    own = blocks_here // chain
    own_pts = own * PTS_BLK
    rim_pts = HALO * PTS_BLK
    window = REACH * PTS_BLK
    g = lax.axis_index("groups")
    b = lax.axis_index("blocks")
    p = lax.axis_index("pairs")
    s = lax.axis_index("sub")

    def position(b, p, s):
        lane = s + lax.rem(p, 2) * (sub - 1 - 2 * s) if split_sub else 0
        along = p * width + lane
        return along + lax.rem(b, 2) * (chain - 1 - 2 * along)

    def device(rank):
        at_b = lax.div(rank, chain)
        q = lax.rem(rank, chain)
        along = q + lax.rem(at_b, 2) * (chain - 1 - 2 * q)
        at_p = lax.div(along, width)
        lane = lax.rem(along, width)
        at_s = lane + lax.rem(at_p, 2) * (sub - 1 - 2 * lane) if split_sub else s
        return (g, at_b, at_p, at_s)

    q = position(b, p, s)
    rank = b * chain + q
    has_next = rank < blocks * chain - 1
    has_prev = rank > 0
    following = device(jnp.minimum(rank + 1, blocks * chain - 1))
    preceding = device(jnp.maximum(rank - 1, 0))
    member = p * sub + s
    members = pairs * sub

    def other(step):
        there = lax.rem(member + step, members)
        return (g, b, lax.div(there, sub), lax.rem(there, sub))

    here = pl.ds(pl.multiple_of(q * own_pts, PTS_BLK), own_pts)
    pts[...] = jnp.zeros_like(pts)
    pts[0:3, 0:own_pts] = coords_ref[:, here]
    vec_a[:, 0:own_pts] = probes_ref[:, here]
    vec_a[:, own_pts:] = jnp.zeros((PROBES, rim_pts), jnp.float32)
    vec_b[:, own_pts:] = jnp.zeros((PROBES, rim_pts), jnp.float32)
    cap = list_ref.shape[1]
    slot_ids = lax.broadcasted_iota(jnp.int32, (1, cap), 1)
    first_of = list_ref[0:1, :]
    key = (first_of - b * blocks_here) * REACH + list_ref[1:2, :] - first_of
    my_keys = keys.at[member]
    my_keys[...] = jnp.full(my_keys.shape, -1, jnp.int32)
    my_keys[0:1, 0:cap] = jnp.where(slot_ids < count_ref[0], key, -1)

    barrier = pltpu.get_barrier_semaphore()
    cross_next = (q == chain - 1) & has_next
    cross_prev = (q == 0) & has_prev
    for step in range(1, members):
        pl.semaphore_signal(barrier, inc=1, device_id=other(step), device_id_type=MESH)

    @pl.when(cross_next)
    def _():
        pl.semaphore_signal(barrier, inc=1, device_id=following, device_id_type=MESH)

    @pl.when(cross_prev)
    def _():
        pl.semaphore_signal(barrier, inc=1, device_id=preceding, device_id_type=MESH)

    greeted = members - 1 + cross_next.astype(jnp.int32) + cross_prev.astype(jnp.int32)
    pl.semaphore_wait(barrier, greeted)

    def rim_copy(buffer, send, recv):
        return pltpu.make_async_remote_copy(
            src_ref=buffer.at[:, pl.ds(0, rim_pts)],
            dst_ref=buffer.at[:, pl.ds(own_pts, rim_pts)],
            send_sem=send,
            recv_sem=recv,
            device_id=preceding,
            device_id_type=MESH,
        )

    def term_copy(order):
        return pltpu.make_async_remote_copy(
            src_ref=acc.at[:, pl.ds(own_pts, rim_pts)],
            dst_ref=arrived,
            send_sem=term_send.at[order],
            recv_sem=term_recv.at[order],
            device_id=following,
            device_id_type=MESH,
        )

    pts_copy = rim_copy(pts, pts_send, pts_recv)
    halo_copies = [
        rim_copy((vec_a, vec_b)[k % 2], halo_send.at[k], halo_recv.at[k]) for k in range(DEG)
    ]
    term_copies = [term_copy(k) for k in range(DEG)]
    key_copies = [
        pltpu.make_async_remote_copy(
            src_ref=my_keys,
            dst_ref=my_keys,
            send_sem=key_send.at[step],
            recv_sem=key_recv.at[step],
            device_id=other(step),
            device_id_type=MESH,
        )
        for step in range(1, members)
    ]

    @pl.when(has_prev)
    def _():
        pts_copy.start()
        halo_copies[0].start()

    for copy in key_copies:
        copy.start()

    row8 = lax.broadcasted_iota(jnp.int32, (8, 1), 0)

    def build_row(i, carry):
        start = pl.multiple_of(i * PTS_BLK, PTS_BLK)
        block_id = b * blocks_here + q * own + i
        middle = block_id.astype(jnp.float32) * 0.5 + 2.0
        centre = jnp.where(row8 == 0, middle, jnp.where(row8 < 3, 1.5, 0.0))
        local = (pts[:, pl.ds(start, window)] - centre) * STRETCH
        norm = jnp.sum(local * local, axis=0, keepdims=True)
        b0, b1, b2 = pieces(jnp.where(row8 == 4, norm, local))
        right = jnp.concatenate(
            [
                jnp.where(row8 == 3, 1.0, b0),
                jnp.where(row8 == 3, 1.0, b1),
                jnp.where(row8 < 3, b0, jnp.where(row8 == 3, 1.0, b2)),
                b1,
                b2,
                b0,
            ],
            0,
        ).astype(jnp.bfloat16)
        a0, a1, a2 = pieces(
            jnp.where(row8 == 3, norm[:, :PTS_BLK], -2.0 * local[:, :PTS_BLK])
        )
        left = jnp.concatenate(
            [
                jnp.where(row8 == 4, 1.0, a0),
                jnp.where(row8 < 3, a0, jnp.where(row8 == 4, 1.0, a1)),
                jnp.where(row8 < 3, a1, jnp.where(row8 == 4, 1.0, a2)),
                jnp.where(row8 < 3, a1, 0.0),
                jnp.where(row8 < 3, a0, 0.0),
                jnp.where(row8 < 3, a2, 0.0),
            ],
            0,
        )
        left = left.T.astype(jnp.bfloat16)
        for d in range(REACH):
            columns = slice(d * PTS_BLK, (d + 1) * PTS_BLK)
            square = jnp.dot(left, right[:, columns], preferred_element_type=jnp.float32)
            square = jnp.maximum(square, 1e-10)
            inside = jnp.maximum(STRETCH - square * lax.rsqrt(square), 0.0)
            inside2 = inside * inside
            tile = (inside2 * inside2) * (1.25 * STRETCH - inside)
            high = tile.astype(jnp.bfloat16)
            tile_hi[i, :, columns] = high
            tile_lo[i, :, columns] = (tile - high.astype(jnp.float32)).astype(jnp.float8_e4m3fn)
        return carry

    inner = own - HALO
    lax.fori_loop(0, inner, build_row, 0)

    @pl.when(has_next)
    def _():
        pts_copy.wait_recv()

    lax.fori_loop(inner, own, build_row, 0)

    for copy in key_copies:
        copy.wait_recv()
    own_rows = lax.broadcasted_iota(jnp.int32, (own, 1), 0)
    for d in range(REACH):
        ids = (q * own + own_rows) * REACH + d
        count = jnp.zeros((own, 1), jnp.float32)
        for m in range(members):
            same = jnp.where(keys[m, 0:1, :] == ids, 1.0, 0.0)
            count = count + jnp.sum(same, axis=1, keepdims=True)
        weights[:, d * PTS_BLK : (d + 1) * PTS_BLK] = jnp.broadcast_to(count, (own, PTS_BLK))

    heaviest = jnp.max(weights[...], axis=(0, 1), keepdims=True)
    heaviest = jnp.maximum(heaviest, 1.0)
    by_last = (((1,), (1,)), ((), ()))

    def apply_rows(current, peak):
        shrink = TOP / jnp.maximum(peak, 1e-30)
        grow = peak * (1.0 / TOP)
        shrink_seen = shrink / heaviest
        grow_seen = grow * heaviest

        def body(i, carry):
            start = pl.multiple_of(i * PTS_BLK, PTS_BLK)
            weight = weights[pl.ds(i, 1), :]
            reach = pl.ds(start, window)
            block = pl.ds(start, PTS_BLK)
            beyond = pl.ds(pl.multiple_of(start + PTS_BLK, PTS_BLK), rim_pts)
            seen = current[:, beyond] * weight[:, PTS_BLK:]
            mine = current[:, block]
            seen_low = (seen * shrink_seen).astype(jnp.float8_e4m3fn)
            mine_low = (mine * shrink).astype(jnp.float8_e4m3fn)
            fwd = lax.dot_general(
                stacked(seen), tile_hi[i, :, PTS_BLK:], by_last, preferred_element_type=jnp.float32
            )
            fwd_low = lax.dot_general(
                seen_low, tile_lo[i, :, PTS_BLK:], by_last, preferred_element_type=jnp.float32
            )
            bwd = jnp.dot(stacked(mine), tile_hi[i], preferred_element_type=jnp.float32)
            bwd_low = jnp.dot(mine_low, tile_lo[i], preferred_element_type=jnp.float32)
            acc[:, reach] += (bwd[:PROBES] + bwd[PROBES:] + bwd_low * grow) * weight
            acc[:, block] += fwd[:PROBES] + fwd[PROBES:] + fwd_low * grow_seen
            return carry

        return body

    def peak_of(value):
        return jnp.max(jnp.abs(value), axis=(0, 1), keepdims=True)

    early = (inner + 1) // 2
    for k in range(DEG):
        current = (vec_a, vec_b)[k % 2]
        before = (vec_b, vec_a)[k % 2]
        peak = peak_of(current[:, 0:own_pts])
        body = apply_rows(current, peak)
        acc[...] = jnp.zeros_like(acc)
        lax.fori_loop(0, early, body, 0)

        @pl.when(has_next)
        def _():
            halo_copies[k].wait_recv()

        peak = jnp.maximum(peak, peak_of(current[:, own_pts:]))
        acc_body = apply_rows(current, peak)
        lax.fori_loop(inner, own, acc_body, 0)

        @pl.when(has_next)
        def _():
            term_copies[k].start()

        lax.fori_loop(early, inner, body, 0)

        @pl.when(has_prev)
        def _():
            halo_copies[k].wait_send()
            term_copies[k].wait_recv()
            acc[:, 0:rim_pts] += arrived[...]

        def advance(lo, hi):
            at = pl.ds(pl.multiple_of(q * own_pts + lo, PTS_BLK), hi - lo)
            value = current[:, lo:hi]
            moved = noise_ref[:, at] * value + acc[:, lo:hi] * (1.0 / TILE_UNIT) - spectrum_center * value
            if k == 0:
                fresh = moved / spectrum_half
                out_ref[:, at] = coeffs_ref[0] * value + coeffs_ref[1] * fresh
            else:
                fresh = moved * (2.0 / spectrum_half) - before[:, lo:hi]
                out_ref[:, at] = out_ref[:, at] + coeffs_ref[k + 1] * fresh
            if k < DEG - 1:
                before[:, lo:hi] = fresh

        advance(0, rim_pts)
        if k < DEG - 1:

            @pl.when(has_prev)
            def _():
                halo_copies[k + 1].start()

        advance(rim_pts, own_pts)

        @pl.when(has_next)
        def _():
            term_copies[k].wait_send()

    @pl.when(has_prev)
    def _():
        pts_copy.wait_send()

    for copy in key_copies:
        copy.wait_send()

    def out_copy(at_p, sem, device_id):
        at_q = position(b, at_p, s)
        part = out_ref.at[:, pl.ds(pl.multiple_of(at_q * own_pts, PTS_BLK), own_pts)]
        return pltpu.make_async_remote_copy(
            src_ref=part,
            dst_ref=part,
            send_sem=out_send.at[sem],
            recv_sem=out_recv.at[sem],
            device_id=device_id,
            device_id_type=MESH,
        )

    across = [out_copy(p, step, (g, b, lax.rem(p + step, pairs), s)) for step in range(1, pairs)]
    for copy in across:
        copy.start()
    inside = []
    if split_sub:
        for step in range(pairs):
            if step > 0:
                across[step - 1].wait_recv()
            source = lax.rem(p + pairs - step, pairs)
            for turn in range(1, sub):
                sem = pairs + step * sub + turn
                copy = out_copy(source, sem, (g, b, p, lax.rem(s + turn, sub)))
                copy.start()
                inside.append(copy)
    else:
        for copy in across:
            copy.wait_recv()
    for copy in inside:
        copy.wait_recv()
    for copy in across + inside:
        copy.wait_send()


def on_device(layout, coords, probes, noise, pair_list, pair_count, coeffs):
    blocks, pairs, sub, split_sub, blocks_here = layout
    own = blocks_here // (pairs * (sub if split_sub else 1))
    members = pairs * sub
    own_pts = own * PTS_BLK
    ext_pts = own_pts + HALO * PTS_BLK
    window = REACH * PTS_BLK
    key_lanes = -(-pair_list.shape[1] // 128) * 128
    dma = pltpu.SemaphoreType.DMA
    vmem = pl.BlockSpec(memory_space=pltpu.VMEM)
    smem = pl.BlockSpec(memory_space=pltpu.SMEM)
    return pl.pallas_call(
        functools.partial(kernel, layout),
        out_shape=jax.ShapeDtypeStruct(probes.shape, jnp.float32),
        in_specs=[vmem, vmem, vmem, vmem, smem, smem],
        out_specs=vmem,
        scratch_shapes=[
            pltpu.VMEM((8, ext_pts), jnp.float32),
            pltpu.VMEM((PROBES, ext_pts), jnp.float32),
            pltpu.VMEM((PROBES, ext_pts), jnp.float32),
            pltpu.VMEM((PROBES, ext_pts), jnp.float32),
            pltpu.VMEM((PROBES, HALO * PTS_BLK), jnp.float32),
            pltpu.VMEM((members, 8, key_lanes), jnp.int32),
            pltpu.VMEM((own, window), jnp.float32),
            pltpu.VMEM((own, PTS_BLK, window), jnp.bfloat16),
            pltpu.VMEM((own, PTS_BLK, window), jnp.float8_e4m3fn),
            dma,
            dma,
            dma((DEG,)),
            dma((DEG,)),
            dma((DEG,)),
            dma((DEG,)),
            dma((members,)),
            dma((members,)),
            dma((pairs + members,)),
            dma((pairs + members,)),
        ],
        compiler_params=pltpu.CompilerParams(
            collective_id=0, has_side_effects=True, vmem_limit_bytes=48 * 1024 * 1024
        ),
    )(coords, probes, noise.reshape(1, -1), pair_list, pair_count, coeffs)


def solution(mesh):
    blocks, pairs, sub = (mesh.shape[axis] for axis in ("blocks", "pairs", "sub"))

    def program(coords, *rest):
        total = coords.shape[1] // PTS_BLK
        blocks_here = total // (mesh.shape["groups"] * blocks)
        split_sub = blocks_here // (pairs * sub) >= REACH
        layout = (blocks, pairs, sub, split_sub, blocks_here)
        return jax.shard_map(
            functools.partial(on_device, layout),
            mesh=mesh,
            in_specs=(
                P(None, ("groups", "blocks")),
                P(None, ("groups", "blocks")),
                P(("groups", "blocks")),
                P(None, ("groups", "blocks", "pairs", "sub")),
                P(("groups", "blocks", "pairs", "sub")),
                P("groups"),
            ),
            out_specs=P(None, ("groups", "blocks")),
            check_vma=False,
        )(coords, *rest)

    return program
```

```python
import functools
import math

import jax
import jax.numpy as jnp
from jax import lax
from jax.experimental import pallas as pl
from jax.experimental.pallas import tpu as pltpu
from jax.sharding import PartitionSpec as P

PTS_BLK = 256
REACH = 8
DEG = 4
HALO = REACH - 1
PROBES = 8

kernel_scale = 0.1
spectrum_center = 1.0
spectrum_half = 2.0

MESH = pl.DeviceIdType.MESH

TILE_UNIT = 2.0**20
STRETCH = (4.0 * kernel_scale * TILE_UNIT) ** 0.2
TOP = 240.0


def rounded(value):
    return value.astype(jnp.bfloat16).astype(jnp.float32)


def pieces(value):
    first = rounded(value)
    second = rounded(value - first)
    return first, second, rounded(value - first - second)


def stacked(value):
    high = rounded(value)
    return jnp.concatenate([high, value - high], 0).astype(jnp.bfloat16)


def kernel(
    layout,
    coords_ref,
    probes_ref,
    noise_ref,
    list_ref,
    count_ref,
    coeffs_ref,
    out_ref,
    pts,
    vec_a,
    vec_b,
    acc,
    arrived,
    keys,
    weights,
    tile_hi,
    tile_lo,
    turned_hi,
    turned_lo,
    pts_send,
    pts_recv,
    halo_send,
    halo_recv,
    term_send,
    term_recv,
    key_send,
    key_recv,
    out_send,
    out_recv,
):
    blocks, pairs, sub, split_sub, blocks_here = layout
    width = sub if split_sub else 1
    chain = pairs * width
    own = blocks_here // chain
    own_pts = own * PTS_BLK
    rim_pts = HALO * PTS_BLK
    window = REACH * PTS_BLK
    g = lax.axis_index("groups")
    b = lax.axis_index("blocks")
    p = lax.axis_index("pairs")
    s = lax.axis_index("sub")

    def position(b, p, s):
        lane = s + lax.rem(p, 2) * (sub - 1 - 2 * s) if split_sub else 0
        along = p * width + lane
        return along + lax.rem(b, 2) * (chain - 1 - 2 * along)

    def device(rank):
        at_b = lax.div(rank, chain)
        q = lax.rem(rank, chain)
        along = q + lax.rem(at_b, 2) * (chain - 1 - 2 * q)
        at_p = lax.div(along, width)
        lane = lax.rem(along, width)
        at_s = lane + lax.rem(at_p, 2) * (sub - 1 - 2 * lane) if split_sub else s
        return (g, at_b, at_p, at_s)

    q = position(b, p, s)
    rank = b * chain + q
    has_next = rank < blocks * chain - 1
    has_prev = rank > 0
    following = device(jnp.minimum(rank + 1, blocks * chain - 1))
    preceding = device(jnp.maximum(rank - 1, 0))
    member = p * sub + s
    members = pairs * sub

    def other(step):
        there = lax.rem(member + step, members)
        return (g, b, lax.div(there, sub), lax.rem(there, sub))

    here = pl.ds(pl.multiple_of(q * own_pts, PTS_BLK), own_pts)
    pts[...] = jnp.zeros_like(pts)
    pts[0:3, 0:own_pts] = coords_ref[:, here]
    vec_a[:, 0:own_pts] = probes_ref[:, here]
    vec_a[:, own_pts:] = jnp.zeros((PROBES, rim_pts), jnp.float32)
    vec_b[:, own_pts:] = jnp.zeros((PROBES, rim_pts), jnp.float32)
    cap = list_ref.shape[1]
    slot_ids = lax.broadcasted_iota(jnp.int32, (1, cap), 1)
    first_of = list_ref[0:1, :]
    key = (first_of - b * blocks_here) * REACH + list_ref[1:2, :] - first_of
    my_keys = keys.at[member]
    my_keys[...] = jnp.full(my_keys.shape, -1, jnp.int32)
    my_keys[0:1, 0:cap] = jnp.where(slot_ids < count_ref[0], key, -1)

    barrier = pltpu.get_barrier_semaphore()
    cross_next = (q == chain - 1) & has_next
    cross_prev = (q == 0) & has_prev
    for step in range(1, members):
        pl.semaphore_signal(barrier, inc=1, device_id=other(step), device_id_type=MESH)

    @pl.when(cross_next)
    def _():
        pl.semaphore_signal(barrier, inc=1, device_id=following, device_id_type=MESH)

    @pl.when(cross_prev)
    def _():
        pl.semaphore_signal(barrier, inc=1, device_id=preceding, device_id_type=MESH)

    greeted = members - 1 + cross_next.astype(jnp.int32) + cross_prev.astype(jnp.int32)
    pl.semaphore_wait(barrier, greeted)

    def rim_copy(buffer, send, recv):
        return pltpu.make_async_remote_copy(
            src_ref=buffer.at[:, pl.ds(0, rim_pts)],
            dst_ref=buffer.at[:, pl.ds(own_pts, rim_pts)],
            send_sem=send,
            recv_sem=recv,
            device_id=preceding,
            device_id_type=MESH,
        )

    def term_copy(order):
        return pltpu.make_async_remote_copy(
            src_ref=acc.at[:, pl.ds(own_pts, rim_pts)],
            dst_ref=arrived,
            send_sem=term_send.at[order],
            recv_sem=term_recv.at[order],
            device_id=following,
            device_id_type=MESH,
        )

    pts_copy = rim_copy(pts, pts_send, pts_recv)
    halo_copies = [
        rim_copy((vec_a, vec_b)[k % 2], halo_send.at[k], halo_recv.at[k]) for k in range(DEG)
    ]
    term_copies = [term_copy(k) for k in range(DEG)]
    key_copies = [
        pltpu.make_async_remote_copy(
            src_ref=my_keys,
            dst_ref=my_keys,
            send_sem=key_send.at[step],
            recv_sem=key_recv.at[step],
            device_id=other(step),
            device_id_type=MESH,
        )
        for step in range(1, members)
    ]

    @pl.when(has_prev)
    def _():
        pts_copy.start()
        halo_copies[0].start()

    for copy in key_copies:
        copy.start()

    row8 = lax.broadcasted_iota(jnp.int32, (8, 1), 0)

    def build_row(i, carry):
        start = pl.multiple_of(i * PTS_BLK, PTS_BLK)
        block_id = b * blocks_here + q * own + i
        middle = block_id.astype(jnp.float32) * 0.5 + 2.0
        centre = jnp.where(row8 == 0, middle, jnp.where(row8 < 3, 1.5, 0.0))
        local = (pts[:, pl.ds(start, window)] - centre) * STRETCH
        norm = jnp.sum(local * local, axis=0, keepdims=True)
        b0, b1, b2 = pieces(jnp.where(row8 == 4, norm, local))
        right = jnp.concatenate(
            [
                jnp.where(row8 == 3, 1.0, b0),
                jnp.where(row8 == 3, 1.0, b1),
                jnp.where(row8 < 3, b0, jnp.where(row8 == 3, 1.0, b2)),
                b1,
                b2,
                b0,
            ],
            0,
        ).astype(jnp.bfloat16)
        a0, a1, a2 = pieces(
            jnp.where(row8 == 3, norm[:, :PTS_BLK], -2.0 * local[:, :PTS_BLK])
        )
        left = jnp.concatenate(
            [
                jnp.where(row8 == 4, 1.0, a0),
                jnp.where(row8 < 3, a0, jnp.where(row8 == 4, 1.0, a1)),
                jnp.where(row8 < 3, a1, jnp.where(row8 == 4, 1.0, a2)),
                jnp.where(row8 < 3, a1, 0.0),
                jnp.where(row8 < 3, a0, 0.0),
                jnp.where(row8 < 3, a2, 0.0),
            ],
            0,
        )
        left = left.T.astype(jnp.bfloat16)
        for d in range(REACH):
            columns = slice(d * PTS_BLK, (d + 1) * PTS_BLK)
            square = jnp.dot(left, right[:, columns], preferred_element_type=jnp.float32)
            square = jnp.maximum(square, 1e-10)
            inside = jnp.maximum(STRETCH - square * lax.rsqrt(square), 0.0)
            inside2 = inside * inside
            tile = (inside2 * inside2) * (1.25 * STRETCH - inside)
            high = tile.astype(jnp.bfloat16)
            tile_hi[i, :, columns] = high
            low = tile - high.astype(jnp.float32)
            tile_lo[i, :, columns] = low.astype(jnp.float8_e4m3fn)
            if d > 0:
                rows = slice((d - 1) * PTS_BLK, d * PTS_BLK)
                turned_hi[i, rows, :] = high.T
                turned_lo[i, rows, :] = low.astype(jnp.bfloat16).T.astype(jnp.float8_e4m3fn)
        return carry

    inner = own - HALO
    lax.fori_loop(0, inner, build_row, 0)

    @pl.when(has_next)
    def _():
        pts_copy.wait_recv()

    lax.fori_loop(inner, own, build_row, 0)

    for copy in key_copies:
        copy.wait_recv()
    own_rows = lax.broadcasted_iota(jnp.int32, (own, 1), 0)
    for d in range(REACH):
        ids = (q * own + own_rows) * REACH + d
        count = jnp.zeros((own, 1), jnp.float32)
        for m in range(members):
            same = jnp.where(keys[m, 0:1, :] == ids, 1.0, 0.0)
            count = count + jnp.sum(same, axis=1, keepdims=True)
        weights[:, d * PTS_BLK : (d + 1) * PTS_BLK] = jnp.broadcast_to(count, (own, PTS_BLK))

    heaviest = jnp.max(weights[...], axis=(0, 1), keepdims=True)
    heaviest = jnp.maximum(heaviest, 1.0)
    group = math.gcd(own, 4)

    def apply_rows(current, peak):
        shrink = TOP / jnp.maximum(peak, 1e-30)
        grow = peak * (1.0 / TOP)
        shrink_seen = shrink / heaviest
        grow_seen = grow * heaviest

        def body(turn, carry):
            found = []
            for step in range(group):
                i = turn * group + step
                start = pl.multiple_of(i * PTS_BLK, PTS_BLK)
                weight = weights[pl.ds(i, 1), :]
                reach = pl.ds(start, window)
                block = pl.ds(start, PTS_BLK)
                beyond = pl.ds(pl.multiple_of(start + PTS_BLK, PTS_BLK), rim_pts)
                seen = current[:, beyond] * weight[:, PTS_BLK:]
                mine = current[:, block]
                seen_low = (seen * shrink_seen).astype(jnp.float8_e4m3fn)
                mine_low = (mine * shrink).astype(jnp.float8_e4m3fn)
                fwd = jnp.dot(stacked(seen), turned_hi[i], preferred_element_type=jnp.float32)
                fwd_low = jnp.dot(seen_low, turned_lo[i], preferred_element_type=jnp.float32)
                bwd = jnp.dot(stacked(mine), tile_hi[i], preferred_element_type=jnp.float32)
                bwd_low = jnp.dot(mine_low, tile_lo[i], preferred_element_type=jnp.float32)
                back = (bwd[:PROBES] + bwd[PROBES:] + bwd_low * grow) * weight
                front = fwd[:PROBES] + fwd[PROBES:] + fwd_low * grow_seen
                found.append((reach, block, back, front))
            for reach, block, back, front in found:
                acc[:, reach] += back
                acc[:, block] += front
            return carry

        return body

    def peak_of(value):
        return jnp.max(jnp.abs(value), axis=(0, 1), keepdims=True)

    rim_turn = inner // group
    late_turns = rim_turn // 2
    parts = [((late_turns * group + HALO) * PTS_BLK, own_pts)]
    middle = (late_turns * group + HALO) // 2 * PTS_BLK
    parts += [(middle, parts[0][0]), (0, middle)]

    def out_copy(at_p, part, sem, device_id):
        lo, hi = parts[part]
        at = position(b, at_p, s) * own_pts + lo
        piece = out_ref.at[:, pl.ds(pl.multiple_of(at, PTS_BLK), hi - lo)]
        return pltpu.make_async_remote_copy(
            src_ref=piece,
            dst_ref=piece,
            send_sem=out_send.at[part, sem],
            recv_sem=out_recv.at[part, sem],
            device_id=device_id,
            device_id_type=MESH,
        )

    across = [
        [out_copy(p, n, step, (g, b, lax.rem(p + step, pairs), s)) for step in range(1, pairs)]
        for n in range(len(parts))
    ]

    def to_sub(n, step):
        source = lax.rem(p + pairs - step, pairs)
        return [
            out_copy(source, n, pairs + step * sub + turn, (g, b, p, lax.rem(s + turn, sub)))
            for turn in range(1, sub if split_sub else 1)
        ]

    inside = [[to_sub(n, step) for step in range(pairs)] for n in range(len(parts))]

    def send_part(n):
        for copy in across[n] + inside[n][0]:
            copy.start()

    for k in range(DEG):
        current = (vec_a, vec_b)[k % 2]
        before = (vec_b, vec_a)[k % 2]
        peak = peak_of(current[:, 0:own_pts])
        body = apply_rows(current, peak)
        acc[...] = jnp.zeros_like(acc)
        lax.fori_loop(late_turns, rim_turn, body, 0)

        @pl.when(has_next)
        def _():
            halo_copies[k].wait_recv()

        peak = jnp.maximum(peak, peak_of(current[:, own_pts:]))
        lax.fori_loop(rim_turn, own // group, apply_rows(current, peak), 0)

        @pl.when(has_next)
        def _():
            term_copies[k].start()

        def advance(lo, hi):
            at = pl.ds(pl.multiple_of(q * own_pts + lo, PTS_BLK), hi - lo)
            value = current[:, lo:hi]
            moved = noise_ref[:, at] * value + acc[:, lo:hi] * (1.0 / TILE_UNIT) - spectrum_center * value
            if k == 0:
                fresh = moved / spectrum_half
                out_ref[:, at] = coeffs_ref[0] * value + coeffs_ref[1] * fresh
            else:
                fresh = moved * (2.0 / spectrum_half) - before[:, lo:hi]
                out_ref[:, at] = out_ref[:, at] + coeffs_ref[k + 1] * fresh
            if k < DEG - 1:
                before[:, lo:hi] = fresh

        if k == DEG - 1:
            advance(*parts[0])
            send_part(0)

        lax.fori_loop(0, late_turns, body, 0)

        @pl.when(has_prev)
        def _():
            halo_copies[k].wait_send()
            term_copies[k].wait_recv()
            acc[:, 0:rim_pts] += arrived[...]

        if k < DEG - 1:
            advance(0, rim_pts)

            @pl.when(has_prev)
            def _():
                halo_copies[k + 1].start()

            advance(rim_pts, own_pts)
        else:
            for n in range(1, len(parts)):
                advance(*parts[n])
                send_part(n)

        @pl.when(has_next)
        def _():
            term_copies[k].wait_send()

    @pl.when(has_prev)
    def _():
        pts_copy.wait_send()

    for copy in key_copies:
        copy.wait_send()

    for n in range(len(parts)):
        for step in range(1, pairs):
            across[n][step - 1].wait_recv()
            for copy in inside[n][step]:
                copy.start()
    for n in range(len(parts)):
        for copies in inside[n]:
            for copy in copies:
                copy.wait()
        for copy in across[n]:
            copy.wait_send()


def on_device(layout, coords, probes, noise, pair_list, pair_count, coeffs):
    blocks, pairs, sub, split_sub, blocks_here = layout
    own = blocks_here // (pairs * (sub if split_sub else 1))
    members = pairs * sub
    own_pts = own * PTS_BLK
    ext_pts = own_pts + HALO * PTS_BLK
    window = REACH * PTS_BLK
    key_lanes = -(-pair_list.shape[1] // 128) * 128
    dma = pltpu.SemaphoreType.DMA
    vmem = pl.BlockSpec(memory_space=pltpu.VMEM)
    smem = pl.BlockSpec(memory_space=pltpu.SMEM)
    return pl.pallas_call(
        functools.partial(kernel, layout),
        out_shape=jax.ShapeDtypeStruct(probes.shape, jnp.float32),
        in_specs=[vmem, vmem, vmem, vmem, smem, smem],
        out_specs=vmem,
        scratch_shapes=[
            pltpu.VMEM((8, ext_pts), jnp.float32),
            pltpu.VMEM((PROBES, ext_pts), jnp.float32),
            pltpu.VMEM((PROBES, ext_pts), jnp.float32),
            pltpu.VMEM((PROBES, ext_pts), jnp.float32),
            pltpu.VMEM((PROBES, HALO * PTS_BLK), jnp.float32),
            pltpu.VMEM((members, 8, key_lanes), jnp.int32),
            pltpu.VMEM((own, window), jnp.float32),
            pltpu.VMEM((own, PTS_BLK, window), jnp.bfloat16),
            pltpu.VMEM((own, PTS_BLK, window), jnp.float8_e4m3fn),
            pltpu.VMEM((own, HALO * PTS_BLK, PTS_BLK), jnp.bfloat16),
            pltpu.VMEM((own, HALO * PTS_BLK, PTS_BLK), jnp.float8_e4m3fn),
            dma,
            dma,
            dma((DEG,)),
            dma((DEG,)),
            dma((DEG,)),
            dma((DEG,)),
            dma((members,)),
            dma((members,)),
            dma((3, pairs + members)),
            dma((3, pairs + members)),
        ],
        compiler_params=pltpu.CompilerParams(
            collective_id=0, has_side_effects=True, vmem_limit_bytes=56 * 1024 * 1024
        ),
    )(coords, probes, noise.reshape(1, -1), pair_list, pair_count, coeffs)


def solution(mesh):
    blocks, pairs, sub = (mesh.shape[axis] for axis in ("blocks", "pairs", "sub"))

    def program(coords, *rest):
        total = coords.shape[1] // PTS_BLK
        blocks_here = total // (mesh.shape["groups"] * blocks)
        split_sub = blocks_here // (pairs * sub) >= REACH
        layout = (blocks, pairs, sub, split_sub, blocks_here)
        return jax.shard_map(
            functools.partial(on_device, layout),
            mesh=mesh,
            in_specs=(
                P(None, ("groups", "blocks")),
                P(None, ("groups", "blocks")),
                P(("groups", "blocks")),
                P(None, ("groups", "blocks", "pairs", "sub")),
                P(("groups", "blocks", "pairs", "sub")),
                P("groups"),
            ),
            out_specs=P(None, ("groups", "blocks")),
            check_vma=False,
        )(coords, *rest)

    return program
```

```python
import functools
import math

import jax
import jax.numpy as jnp
from jax import lax
from jax.experimental import pallas as pl
from jax.experimental.pallas import tpu as pltpu
from jax.sharding import PartitionSpec as P

PTS_BLK = 256
REACH = 8
DEG = 4
HALO = REACH - 1
PROBES = 8

kernel_scale = 0.1
spectrum_center = 1.0
spectrum_half = 2.0

MESH = pl.DeviceIdType.MESH

TILE_UNIT = 2.0**20
STRETCH = (4.0 * kernel_scale * TILE_UNIT) ** 0.2
TOP = 240.0


def rounded(value):
    return value.astype(jnp.bfloat16).astype(jnp.float32)


def pieces(value):
    first = rounded(value)
    second = rounded(value - first)
    return first, second, rounded(value - first - second)


def stacked(value):
    high = rounded(value)
    return jnp.concatenate([high, value - high], 0).astype(jnp.bfloat16)


def kernel(
    layout,
    coords_ref,
    probes_ref,
    noise_ref,
    list_ref,
    count_ref,
    coeffs_ref,
    out_ref,
    pts,
    vec_a,
    vec_b,
    acc,
    arrived,
    keys,
    weights,
    tile_hi,
    tile_lo,
    turned_hi,
    turned_lo,
    pts_send,
    pts_recv,
    halo_send,
    halo_recv,
    term_send,
    term_recv,
    key_send,
    key_recv,
    out_send,
    out_recv,
):
    blocks, pairs, sub, split_sub, blocks_here = layout
    width = sub if split_sub else 1
    chain = pairs * width
    own = blocks_here // chain
    own_pts = own * PTS_BLK
    rim_pts = HALO * PTS_BLK
    window = REACH * PTS_BLK
    g = lax.axis_index("groups")
    b = lax.axis_index("blocks")
    p = lax.axis_index("pairs")
    s = lax.axis_index("sub")

    def position(b, p, s):
        lane = s + lax.rem(p, 2) * (sub - 1 - 2 * s) if split_sub else 0
        along = p * width + lane
        return along + lax.rem(b, 2) * (chain - 1 - 2 * along)

    def device(rank):
        at_b = lax.div(rank, chain)
        q = lax.rem(rank, chain)
        along = q + lax.rem(at_b, 2) * (chain - 1 - 2 * q)
        at_p = lax.div(along, width)
        lane = lax.rem(along, width)
        at_s = lane + lax.rem(at_p, 2) * (sub - 1 - 2 * lane) if split_sub else s
        return (g, at_b, at_p, at_s)

    q = position(b, p, s)
    rank = b * chain + q
    has_next = rank < blocks * chain - 1
    has_prev = rank > 0
    following = device(jnp.minimum(rank + 1, blocks * chain - 1))
    preceding = device(jnp.maximum(rank - 1, 0))
    member = p * sub + s
    members = pairs * sub

    def other(step):
        there = lax.rem(member + step, members)
        return (g, b, lax.div(there, sub), lax.rem(there, sub))

    here = pl.ds(pl.multiple_of(q * own_pts, PTS_BLK), own_pts)
    pts[...] = jnp.zeros_like(pts)
    pts[0:3, 0:own_pts] = coords_ref[:, here]
    vec_a[:, 0:own_pts] = probes_ref[:, here]
    vec_a[:, own_pts:] = jnp.zeros((PROBES, rim_pts), jnp.float32)
    vec_b[:, own_pts:] = jnp.zeros((PROBES, rim_pts), jnp.float32)
    cap = list_ref.shape[1]
    slot_ids = lax.broadcasted_iota(jnp.int32, (1, cap), 1)
    first_of = list_ref[0:1, :]
    key = (first_of - b * blocks_here) * REACH + list_ref[1:2, :] - first_of
    my_keys = keys.at[member]
    my_keys[...] = jnp.full(my_keys.shape, -1, jnp.int32)
    my_keys[0:1, 0:cap] = jnp.where(slot_ids < count_ref[0], key, -1)

    barrier = pltpu.get_barrier_semaphore()
    cross_next = (q == chain - 1) & has_next
    cross_prev = (q == 0) & has_prev
    for step in range(1, members):
        pl.semaphore_signal(barrier, inc=1, device_id=other(step), device_id_type=MESH)

    @pl.when(cross_next)
    def _():
        pl.semaphore_signal(barrier, inc=1, device_id=following, device_id_type=MESH)

    @pl.when(cross_prev)
    def _():
        pl.semaphore_signal(barrier, inc=1, device_id=preceding, device_id_type=MESH)

    greeted = members - 1 + cross_next.astype(jnp.int32) + cross_prev.astype(jnp.int32)
    pl.semaphore_wait(barrier, greeted)

    def rim_copy(buffer, send, recv):
        return pltpu.make_async_remote_copy(
            src_ref=buffer.at[:, pl.ds(0, rim_pts)],
            dst_ref=buffer.at[:, pl.ds(own_pts, rim_pts)],
            send_sem=send,
            recv_sem=recv,
            device_id=preceding,
            device_id_type=MESH,
        )

    def term_copy(order):
        return pltpu.make_async_remote_copy(
            src_ref=acc.at[:, pl.ds(own_pts, rim_pts)],
            dst_ref=arrived,
            send_sem=term_send.at[order],
            recv_sem=term_recv.at[order],
            device_id=following,
            device_id_type=MESH,
        )

    pts_copy = rim_copy(pts, pts_send, pts_recv)
    halo_copies = [
        rim_copy((vec_a, vec_b)[k % 2], halo_send.at[k], halo_recv.at[k]) for k in range(DEG)
    ]
    term_copies = [term_copy(k) for k in range(DEG)]
    key_copies = [
        pltpu.make_async_remote_copy(
            src_ref=my_keys,
            dst_ref=my_keys,
            send_sem=key_send.at[step],
            recv_sem=key_recv.at[step],
            device_id=other(step),
            device_id_type=MESH,
        )
        for step in range(1, members)
    ]

    @pl.when(has_prev)
    def _():
        pts_copy.start()
        halo_copies[0].start()

    for copy in key_copies:
        copy.start()

    row8 = lax.broadcasted_iota(jnp.int32, (8, 1), 0)

    def build_row(i, carry):
        start = pl.multiple_of(i * PTS_BLK, PTS_BLK)
        block_id = b * blocks_here + q * own + i
        middle = block_id.astype(jnp.float32) * 0.5 + 2.0
        centre = jnp.where(row8 == 0, middle, jnp.where(row8 < 3, 1.5, 0.0))
        local = (pts[:, pl.ds(start, window)] - centre) * STRETCH
        norm = jnp.sum(local * local, axis=0, keepdims=True)
        b0, b1, b2 = pieces(jnp.where(row8 == 4, norm, local))
        right = jnp.concatenate(
            [
                jnp.where(row8 == 3, 1.0, b0),
                jnp.where(row8 == 3, 1.0, b1),
                jnp.where(row8 < 3, b0, jnp.where(row8 == 3, 1.0, b2)),
                b1,
                b2,
                b0,
            ],
            0,
        ).astype(jnp.bfloat16)
        a0, a1, a2 = pieces(
            jnp.where(row8 == 3, norm[:, :PTS_BLK], -2.0 * local[:, :PTS_BLK])
        )
        left = jnp.concatenate(
            [
                jnp.where(row8 == 4, 1.0, a0),
                jnp.where(row8 < 3, a0, jnp.where(row8 == 4, 1.0, a1)),
                jnp.where(row8 < 3, a1, jnp.where(row8 == 4, 1.0, a2)),
                jnp.where(row8 < 3, a1, 0.0),
                jnp.where(row8 < 3, a0, 0.0),
                jnp.where(row8 < 3, a2, 0.0),
            ],
            0,
        )
        left = left.T.astype(jnp.bfloat16)
        for d in range(REACH):
            columns = slice(d * PTS_BLK, (d + 1) * PTS_BLK)
            square = jnp.dot(left, right[:, columns], preferred_element_type=jnp.float32)
            square = jnp.maximum(square, 1e-10)
            inside = jnp.maximum(STRETCH - square * lax.rsqrt(square), 0.0)
            inside2 = inside * inside
            tile = (inside2 * inside2) * (1.25 * STRETCH - inside)
            high = tile.astype(jnp.bfloat16)
            tile_hi[i, :, columns] = high
            low = tile - high.astype(jnp.float32)
            tile_lo[i, :, columns] = low.astype(jnp.float8_e4m3fn)
            if d > 0:
                rows = slice((d - 1) * PTS_BLK, d * PTS_BLK)
                turned = tile.T
                high = turned.astype(jnp.bfloat16)
                low = turned - high.astype(jnp.float32)
                turned_hi[i, rows, :] = high
                turned_lo[i, rows, :] = low.astype(jnp.float8_e4m3fn)
        return carry

    inner = own - HALO
    lax.fori_loop(0, inner, build_row, 0)

    @pl.when(has_next)
    def _():
        pts_copy.wait_recv()

    lax.fori_loop(inner, own, build_row, 0)

    for copy in key_copies:
        copy.wait_recv()
    own_rows = lax.broadcasted_iota(jnp.int32, (own, 1), 0)
    for d in range(REACH):
        ids = (q * own + own_rows) * REACH + d
        count = jnp.zeros((own, 1), jnp.float32)
        for m in range(members):
            same = jnp.where(keys[m, 0:1, :] == ids, 1.0, 0.0)
            count = count + jnp.sum(same, axis=1, keepdims=True)
        weights[:, d * PTS_BLK : (d + 1) * PTS_BLK] = jnp.broadcast_to(count, (own, PTS_BLK))

    heaviest = jnp.max(weights[...], axis=(0, 1), keepdims=True)
    heaviest = jnp.maximum(heaviest, 1.0)
    group = math.gcd(own, 4)

    def apply_rows(current, peak):
        shrink = TOP / jnp.maximum(peak, 1e-30)
        grow = peak * (1.0 / TOP)
        shrink_seen = shrink / heaviest
        grow_seen = grow * heaviest

        def row_terms(i, lo, hi):
            start = i * PTS_BLK
            if not isinstance(i, int):
                start = pl.multiple_of(start, PTS_BLK)
            weight = weights[pl.ds(i, 1), :]
            block = pl.ds(start, PTS_BLK)
            reach = pl.ds(start + lo * PTS_BLK, (hi - lo) * PTS_BLK)
            mine = current[:, block]
            mine_low = (mine * shrink).astype(jnp.float8_e4m3fn)
            met = slice(lo * PTS_BLK, hi * PTS_BLK)
            bwd = jnp.dot(stacked(mine), tile_hi[i, :, met], preferred_element_type=jnp.float32)
            bwd_low = jnp.dot(mine_low, tile_lo[i, :, met], preferred_element_type=jnp.float32)
            back = (bwd[:PROBES] + bwd[PROBES:] + bwd_low * grow) * weight[:, met]
            first = max(lo, 1)
            if first == hi:
                return reach, block, back, None
            beyond = pl.ds(start + first * PTS_BLK, (hi - first) * PTS_BLK)
            seen = current[:, beyond] * weight[:, first * PTS_BLK : hi * PTS_BLK]
            seen_low = (seen * shrink_seen).astype(jnp.float8_e4m3fn)
            met = slice((first - 1) * PTS_BLK, (hi - 1) * PTS_BLK)
            fwd = jnp.dot(stacked(seen), turned_hi[i, met, :], preferred_element_type=jnp.float32)
            fwd_low = jnp.dot(seen_low, turned_lo[i, met, :], preferred_element_type=jnp.float32)
            front = fwd[:PROBES] + fwd[PROBES:] + fwd_low * grow_seen
            return reach, block, back, front

        def add(found):
            for reach, block, back, front in found:
                acc[:, reach] += back
                if front is not None:
                    acc[:, block] += front

        def body(turn, carry):
            add([row_terms(turn * group + step, 0, REACH) for step in range(group)])
            return carry

        def near():
            for half in range(0, REACH, group):
                rows = range(half, half + group)
                add([row_terms(own - REACH + row, 0, REACH - row) for row in rows])

        def far():
            add([row_terms(own - REACH + row, REACH - row, REACH) for row in range(1, 4)])
            add([row_terms(own - REACH + row, REACH - row, REACH) for row in range(4, REACH)])

        return body, near, far

    def peak_of(value):
        return jnp.max(jnp.abs(value), axis=(0, 1), keepdims=True)

    late_turns = (own - REACH) // group
    parts = [((late_turns * group + HALO) * PTS_BLK, own_pts)]
    middle = (late_turns * group + HALO) // 2 * PTS_BLK
    parts += [(middle, parts[0][0]), (0, middle)]

    def out_copy(at_p, part, sem, device_id):
        lo, hi = parts[part]
        at = position(b, at_p, s) * own_pts + lo
        piece = out_ref.at[:, pl.ds(pl.multiple_of(at, PTS_BLK), hi - lo)]
        return pltpu.make_async_remote_copy(
            src_ref=piece,
            dst_ref=piece,
            send_sem=out_send.at[part, sem],
            recv_sem=out_recv.at[part, sem],
            device_id=device_id,
            device_id_type=MESH,
        )

    across = [
        [out_copy(p, n, step, (g, b, lax.rem(p + step, pairs), s)) for step in range(1, pairs)]
        for n in range(len(parts))
    ]

    def to_sub(n, step):
        source = lax.rem(p + pairs - step, pairs)
        return [
            out_copy(source, n, pairs + step * sub + turn, (g, b, p, lax.rem(s + turn, sub)))
            for turn in range(1, sub if split_sub else 1)
        ]

    inside = [[to_sub(n, step) for step in range(pairs)] for n in range(len(parts))]

    def send_part(n):
        for copy in across[n] + inside[n][0]:
            copy.start()

    for k in range(DEG):
        current = (vec_a, vec_b)[k % 2]
        before = (vec_b, vec_a)[k % 2]
        peak = peak_of(current[:, 0:own_pts])
        body, near, _ = apply_rows(current, peak)
        acc[...] = jnp.zeros_like(acc)
        near()

        @pl.when(has_next)
        def _():
            halo_copies[k].wait_recv()

        peak = jnp.maximum(peak, peak_of(current[:, own_pts:]))
        _, _, far = apply_rows(current, peak)
        far()

        @pl.when(has_next)
        def _():
            term_copies[k].start()

        def advance(lo, hi):
            at = pl.ds(pl.multiple_of(q * own_pts + lo, PTS_BLK), hi - lo)
            value = current[:, lo:hi]
            moved = noise_ref[:, at] * value + acc[:, lo:hi] * (1.0 / TILE_UNIT) - spectrum_center * value
            if k == 0:
                fresh = moved / spectrum_half
                out_ref[:, at] = coeffs_ref[0] * value + coeffs_ref[1] * fresh
            else:
                fresh = moved * (2.0 / spectrum_half) - before[:, lo:hi]
                out_ref[:, at] = out_ref[:, at] + coeffs_ref[k + 1] * fresh
            if k < DEG - 1:
                before[:, lo:hi] = fresh

        if k == DEG - 1:
            advance(*parts[0])
            send_part(0)

        lax.fori_loop(0, late_turns, body, 0)

        @pl.when(has_prev)
        def _():
            halo_copies[k].wait_send()
            term_copies[k].wait_recv()
            acc[:, 0:rim_pts] += arrived[...]

        if k < DEG - 1:
            advance(0, rim_pts)

            @pl.when(has_prev)
            def _():
                halo_copies[k + 1].start()

            advance(rim_pts, own_pts)
        else:
            for n in range(1, len(parts)):
                advance(*parts[n])
                send_part(n)

        @pl.when(has_next)
        def _():
            term_copies[k].wait_send()

    @pl.when(has_prev)
    def _():
        pts_copy.wait_send()

    for copy in key_copies:
        copy.wait_send()

    for n in range(len(parts)):
        for step in range(1, pairs):
            across[n][step - 1].wait_recv()
            for copy in inside[n][step]:
                copy.start()
    for n in range(len(parts)):
        for copies in inside[n]:
            for copy in copies:
                copy.wait()
        for copy in across[n]:
            copy.wait_send()


def on_device(layout, coords, probes, noise, pair_list, pair_count, coeffs):
    blocks, pairs, sub, split_sub, blocks_here = layout
    own = blocks_here // (pairs * (sub if split_sub else 1))
    members = pairs * sub
    own_pts = own * PTS_BLK
    ext_pts = own_pts + HALO * PTS_BLK
    window = REACH * PTS_BLK
    key_lanes = -(-pair_list.shape[1] // 128) * 128
    dma = pltpu.SemaphoreType.DMA
    vmem = pl.BlockSpec(memory_space=pltpu.VMEM)
    smem = pl.BlockSpec(memory_space=pltpu.SMEM)
    return pl.pallas_call(
        functools.partial(kernel, layout),
        out_shape=jax.ShapeDtypeStruct(probes.shape, jnp.float32),
        in_specs=[vmem, vmem, vmem, vmem, smem, smem],
        out_specs=vmem,
        scratch_shapes=[
            pltpu.VMEM((8, ext_pts), jnp.float32),
            pltpu.VMEM((PROBES, ext_pts), jnp.float32),
            pltpu.VMEM((PROBES, ext_pts), jnp.float32),
            pltpu.VMEM((PROBES, ext_pts), jnp.float32),
            pltpu.VMEM((PROBES, HALO * PTS_BLK), jnp.float32),
            pltpu.VMEM((members, 8, key_lanes), jnp.int32),
            pltpu.VMEM((own, window), jnp.float32),
            pltpu.VMEM((own, PTS_BLK, window), jnp.bfloat16),
            pltpu.VMEM((own, PTS_BLK, window), jnp.float8_e4m3fn),
            pltpu.VMEM((own, HALO * PTS_BLK, PTS_BLK), jnp.bfloat16),
            pltpu.VMEM((own, HALO * PTS_BLK, PTS_BLK), jnp.float8_e4m3fn),
            dma,
            dma,
            dma((DEG,)),
            dma((DEG,)),
            dma((DEG,)),
            dma((DEG,)),
            dma((members,)),
            dma((members,)),
            dma((3, pairs + members)),
            dma((3, pairs + members)),
        ],
        compiler_params=pltpu.CompilerParams(
            collective_id=0, has_side_effects=True, vmem_limit_bytes=56 * 1024 * 1024
        ),
    )(coords, probes, noise.reshape(1, -1), pair_list, pair_count, coeffs)


def solution(mesh):
    blocks, pairs, sub = (mesh.shape[axis] for axis in ("blocks", "pairs", "sub"))

    def program(coords, *rest):
        total = coords.shape[1] // PTS_BLK
        blocks_here = total // (mesh.shape["groups"] * blocks)
        split_sub = blocks_here // (pairs * sub) >= REACH
        layout = (blocks, pairs, sub, split_sub, blocks_here)
        return jax.shard_map(
            functools.partial(on_device, layout),
            mesh=mesh,
            in_specs=(
                P(None, ("groups", "blocks")),
                P(None, ("groups", "blocks")),
                P(("groups", "blocks")),
                P(None, ("groups", "blocks", "pairs", "sub")),
                P(("groups", "blocks", "pairs", "sub")),
                P("groups"),
            ),
            out_specs=P(None, ("groups", "blocks")),
            check_vma=False,
        )(coords, *rest)

    return program
```
